256 devices in a mesh: span: 8 (over y, core), seq: 16 (over z_hi, x), mp: 2 (over z_lo).
Axes of the slice: x: 4, y: 4, z: 8 (z_hi: 4, z_lo: 2; z = z_hi * 2 + z_lo), core: 2. Of those that a mesh axis runs over, the one named last changes fastest.
Arguments:
- query: bfloat16 [8, 1024, 4096], P('span', 'seq', 'mp'), may hold values from -33 to 33, as said below
- key: bfloat16 [8, 1024, 4096], P('span', 'seq', 'mp'), may hold values from -33 to 33, as said below
- value: bfloat16 [8, 1024, 4096], P('span', 'seq', 'mp'), may hold values from -6 to 6
- cache_key: bfloat16 [8, 1024, 4096], P('span', 'seq', 'mp'), may hold values from -21 to 21
- cache_value: bfloat16 [8, 1024, 4096], P('span', 'seq', 'mp'), may hold values from -6 to 6
- q_gain: float32 [4096], P('mp'), may hold values from 0.1 to 1.9
- k_gain: float32 [4096], P('mp'), may hold values from 0.1 to 1.9
- gate_table: float32 [32, 4096], P(None, 'mp'), may hold values from 0.5 to 2
- span_order: int32 [8], replicated, may hold values from 0 to 31, as said below
- noise_step: int32 [8], replicated, may hold values from 0 to 31
- context_mask: int32 [32, 32], replicated, may hold values 0 or 1
Outputs:
- attended: bfloat16 [8, 1024, 4096], P('span', 'seq', 'mp')
The draws below stay inside these ranges and needn't reach their ends.
Inputs may be any that keep to these rules, and one draw needn't show every extreme that they name: `query`: rows and columns carry different scales. `key`: rows and columns carry different scales. `span_order`: distinct positions.
All inputs are finite; a program needn't handle non-finite values.
Results may differ from the reference program's by a relative error of at most 0.018.
Values may be sent and summed in bfloat16 or wider, within the bound.
A program may use at most 128 MiB of HBM per device.

```python
import jax
import jax.numpy as jnp
from jax import lax

HEADS = 32
HD = 128
STEPS = 32
SPANS = 8
POSITIONS = 32
SPAN_LEN = 1024
W = 4096


def row_col_scales(key, col_top):
    rows = 0.3 * 10.0 ** jax.random.uniform(key, (SPANS, SPAN_LEN, 1), jnp.float32)
    cols = 0.7 * col_top ** (jnp.arange(W, dtype=jnp.float32) / W)
    return rows * cols[None, None, :]


def draw_query(key, part):
    key = jax.random.fold_in(key, 1)
    first, second = jax.random.split(key)
    shape = (SPANS, SPAN_LEN, W)
    base = jnp.clip(jax.random.normal(first, shape, jnp.float32), -4.0, 4.0)
    result = base * row_col_scales(second, 3.0)
    return result.astype(jnp.bfloat16)


def draw_key(key, part):
    key = jax.random.fold_in(key, 2)
    first, second = jax.random.split(key)
    shape = (SPANS, SPAN_LEN, W)
    base = jnp.clip(jax.random.normal(first, shape, jnp.float32), -4.0, 4.0)
    result = base * row_col_scales(second, 3.0)
    return result.astype(jnp.bfloat16)


def draw_cache_key(key, part):
    key = jax.random.fold_in(key, 3)
    first = jax.random.fold_in(key, 0)
    shape = (SPANS, SPAN_LEN, W)
    result = jnp.clip(jax.random.normal(first, shape, jnp.float32), -4.0, 4.0)
    return result.astype(jnp.bfloat16)


def draw_span_order(key, part):
    key = jax.random.fold_in(key, 4)
    shuffled = jax.random.permutation(key, jnp.arange(POSITIONS, dtype=jnp.int32))[:SPANS]
    lowest = jnp.min(shuffled)
    highest = jnp.max(shuffled)
    result = jnp.where(shuffled == lowest, 0, jnp.where(shuffled == highest, POSITIONS - 1, shuffled))
    return result.astype(jnp.int32)


def with_ends(values, key, least, high):
    longest = values.shape.index(max(values.shape))
    spots = []
    for shift in (0, 1):
        where = [jax.random.randint(jax.random.fold_in(key, axis), (), 0, length) for axis, length in enumerate(values.shape)]
        where[longest] = (where[longest] + shift) % values.shape[longest]
        spots.append(tuple(where))
    return values.at[spots[0]].set(least).at[spots[1]].set(high)


def block_levels(own_key, extent, cuts, low, largest):
    factor_of = 1.0
    for dim, shards_of in cuts:
        draws = jax.random.uniform(jax.random.fold_in(jax.random.fold_in(own_key, 6), dim), (shards_of,), jnp.float32, low / len(cuts), largest / len(cuts))
        factor_of = factor_of * jnp.repeat(jnp.exp(draws), extent[dim] // shards_of).reshape((-1,) + (1,) * (len(extent) - 1 - dim))
    return factor_of


def scatter_about(own_key, extent, spread, most, pieces=(), kind=jnp.bfloat16):
    drawn = spread * jax.random.normal(own_key, extent, jnp.float32)
    if pieces:
        drawn = drawn * block_levels(own_key, extent, pieces, -0.22, 0.18)
    return jnp.clip(drawn, -most, most).astype(kind)


def setup_inputs(seed: int = 0) -> dict:
    streams_of = jax.random.split(jax.random.key(seed), 12)
    query = draw_query(jax.random.fold_in(streams_of[11], 71), 0)
    key = draw_key(jax.random.fold_in(streams_of[11], 71), 0)
    value = scatter_about(streams_of[2], (SPANS, SPAN_LEN, W), 1.0, 6.0, ((0, 8), (1, 16), (2, 2)))
    cache_key = draw_cache_key(jax.random.fold_in(streams_of[11], 71), 0)
    cache_value = scatter_about(streams_of[4], (SPANS, SPAN_LEN, W), 1.0, 6.0, ((0, 8), (1, 16), (2, 2)))
    q_gain = jnp.clip(1.0 + 0.18 * jax.random.normal(streams_of[5], (W,), jnp.float32), 0.1, 1.9)
    k_gain = jnp.clip(1.0 + 0.18 * jax.random.normal(streams_of[6], (W,), jnp.float32), 0.1, 1.9)
    gate_table = jnp.clip(0.5 + 1.5 * jax.random.uniform(streams_of[7], (STEPS, W), jnp.float32) ** block_levels(streams_of[7], (STEPS, W), ((1, 2),), -0.2, 0.2), 0.5, 2.0)
    span_order = draw_span_order(jax.random.fold_in(streams_of[11], 71), 0)
    noise_step = with_ends(jax.random.randint(streams_of[9], (SPANS,), 0, STEPS), jax.random.fold_in(streams_of[9], 1), 0, STEPS - 1).astype(jnp.int32)
    context_mask = with_ends((jax.random.randint(streams_of[10], (POSITIONS, POSITIONS), 0, 4) < 3).astype(jnp.int32), jax.random.fold_in(streams_of[10], 1), 0, 1)
    return dict(query=query, key=key, value=value, cache_key=cache_key, cache_value=cache_value, q_gain=q_gain, k_gain=k_gain, gate_table=gate_table, span_order=span_order, noise_step=noise_step, context_mask=context_mask)


def normed(x, gain):
    x32 = x.astype(jnp.float32)
    factor = lax.rsqrt(lax.optimization_barrier(jnp.mean(x32 * x32, axis=-1, keepdims=True)) + 1e-06)
    return (x32 * factor * gain).astype(jnp.bfloat16)

def reference(query, key, value, cache_key, cache_value, q_gain, k_gain, gate_table, span_order, noise_step, context_mask):
    scale = HD ** (-0.5)
    q_normed = normed(query, q_gain).reshape(SPANS, SPAN_LEN, HEADS, HD)
    k_normed = normed(key, k_gain).reshape(SPANS, SPAN_LEN, HEADS, HD)
    values = value.reshape(SPANS, SPAN_LEN, HEADS, HD)
    cached_keys = cache_key.reshape(SPANS, SPAN_LEN, HEADS, HD)
    cached_values = cache_value.reshape(SPANS, SPAN_LEN, HEADS, HD)
    order = span_order
    visible = (order[None, :] < order[:, None]) & (context_mask[order[:, None], order[None, :]] > 0)
    results = []
    for group in range(SPANS):
        queries = q_normed[group].astype(jnp.float32)

        def scores(block):
            return jnp.einsum('qhd,khd->hqk', queries, block.astype(jnp.float32)) * scale
        own_scores = scores(k_normed[group])
        top_own = lax.optimization_barrier(jnp.max(own_scores, axis=-1))

        def grow(top, other):
            top = lax.cond(visible[group, other], lambda cur: jnp.maximum(cur, lax.optimization_barrier(jnp.max(scores(cached_keys[other]), axis=-1))), lambda cur: cur, top)
            return (top, None)
        top, unused = lax.scan(grow, top_own, jnp.arange(SPANS))

        def weigh(block_scores, block_values):
            weights = jnp.exp(block_scores - top[:, :, None])
            rounded = lax.optimization_barrier(weights.astype(jnp.bfloat16)).astype(jnp.float32)
            numer = jnp.einsum('hqk,khd->hqd', rounded, block_values.astype(jnp.float32))
            return (numer, lax.optimization_barrier(jnp.sum(weights, axis=-1)))
        numer, denom = weigh(own_scores, values[group])

        def accumulate(carry, other):

            def take(cur):
                extra_numer, extra_denom = weigh(scores(cached_keys[other]), cached_values[other])
                return (cur[0] + extra_numer, cur[1] + extra_denom)
            carry = lax.cond(visible[group, other], take, lambda cur: cur, carry)
            return (carry, None)
        (numer, denom), unused = lax.scan(accumulate, (numer, denom), jnp.arange(SPANS))
        heads_out = jnp.transpose(numer / denom[:, :, None], (1, 0, 2))
        factor = lax.rsqrt(lax.optimization_barrier(jnp.mean(heads_out * heads_out, axis=-1, keepdims=True)) + 1e-06)
        gate = gate_table[noise_step[group]].reshape(HEADS, HD)
        results.append((heads_out * factor * gate).astype(jnp.bfloat16).reshape(SPAN_LEN, HEADS * HD))
    return jnp.stack(results)
```

```python
import functools
import math

import jax
import jax.numpy as jnp
from jax import lax
from jax.experimental import pallas as pl
from jax.experimental.pallas import tpu as pltpu
from jax.sharding import PartitionSpec as P

MESH = pl.DeviceIdType.MESH
HEADS = 32
HD = 128
EPS = 1e-6
OUT_OF_MAX = 1e30
OUT_OF_SUM = 3e30


def exchange_and_attend(
    chips_y,
    ring_z,
    ring_x,
    query,
    key,
    value,
    cache_key,
    cache_value,
    q_gain,
    k_gain,
    gate_table,
    span_order,
    noise_step,
    context_mask,
    out,
    raw,
    normed,
    squares,
    gates,
    heads,
    cached,
    total,
    top,
    mass,
    done,
    load_sem,
    local_sem,
    mp_send,
    mp_recv,
    cache_send,
    cache_recv,
    head_send,
    head_recv,
    y_send,
    y_recv,
    core_send,
    core_recv,
    out_send,
    out_recv,
):
    span = lax.axis_index("span")
    seq = lax.axis_index("seq")
    mp = lax.axis_index("mp")
    y, core = span // 2, span % 2
    z, x = seq // ring_x, seq % ring_x
    members = ring_z * ring_x
    tokens = raw.shape[1]
    group = ring_x * tokens
    length = members * tokens
    width = HEADS * HD
    partner = (y * 2 + (1 - core), seq, mp)
    my_rows = pl.ds(pl.multiple_of(seq * tokens, tokens), tokens)
    my_columns = pl.ds(pl.multiple_of(seq * HD, HD), HD)

    def peer(dz, dx):
        return lax.rem(z + dz, ring_z) * ring_x + lax.rem(x + dx, ring_x)

    def group_rows(dz):
        return pl.ds(pl.multiple_of(lax.rem(z + ring_z - dz, ring_z) * group, group), group)

    barrier = pltpu.get_barrier_semaphore()

    def greet(step, carry):
        other = lax.rem(seq + step, members)
        pl.semaphore_signal(barrier, inc=1, device_id=(span, other, mp), device_id_type=MESH)
        return carry

    lax.fori_loop(1, members, greet, 0)
    for dy in range(1, chips_y):
        pl.semaphore_signal(
            barrier,
            inc=1,
            device_id=(lax.rem(y + dy, chips_y) * 2 + core, seq, mp),
            device_id_type=MESH,
        )
    pl.semaphore_signal(barrier, inc=1, device_id=partner, device_id_type=MESH)
    pl.semaphore_signal(barrier, inc=1, device_id=(span, seq, 1 - mp), device_id_type=MESH)

    loads = [
        pltpu.make_async_copy(query.at[0], raw.at[0], load_sem.at[0]),
        pltpu.make_async_copy(key.at[0], raw.at[1], load_sem.at[1]),
        pltpu.make_async_copy(gate_table.at[:, my_columns], gates, load_sem.at[2]),
    ]
    for load in loads:
        load.start()
    owns = [
        pltpu.make_async_copy(
            cache_key.at[0, :, my_columns], cached.at[0, 0, my_rows], local_sem.at[0]
        ),
        pltpu.make_async_copy(
            cache_value.at[0, :, my_columns], cached.at[0, 1, my_rows], local_sem.at[1]
        ),
        pltpu.make_async_copy(value.at[0, :, my_columns], heads.at[2, my_rows], local_sem.at[2]),
    ]
    for own in owns:
        own.start()
    pl.semaphore_wait(barrier, members - 1 + chips_y - 1 + 2)

    for dz in range(ring_z):

        def send_cache(dx, carry, dz=dz):
            other = peer(dz, dx)
            columns = pl.ds(pl.multiple_of(other * HD, HD), HD)
            for which, source in enumerate((cache_key, cache_value)):
                pltpu.make_async_remote_copy(
                    src_ref=source.at[0, :, columns],
                    dst_ref=cached.at[0, which, my_rows],
                    send_sem=cache_send.at[which],
                    recv_sem=cache_recv.at[dz],
                    device_id=(span, other, mp),
                    device_id_type=MESH,
                ).start()
            return carry

        lax.fori_loop(1 if dz == 0 else 0, ring_x, send_cache, 0)

    loads[0].wait()
    loads[1].wait()
    lane = lax.broadcasted_iota(jnp.int32, (tokens, HD), 1)

    def row_squares(which):
        wide = raw[which].astype(jnp.float32)
        return jnp.sum(wide * wide, axis=-1, keepdims=True)

    squares[0] = jnp.where(lane < HD // 2, row_squares(0), row_squares(1))
    swap = pltpu.make_async_remote_copy(
        src_ref=squares.at[0],
        dst_ref=squares.at[1],
        send_sem=mp_send,
        recv_sem=mp_recv,
        device_id=(span, seq, 1 - mp),
        device_id_type=MESH,
    )
    swap.start()
    swap.wait()
    factors = lax.rsqrt((squares[0] + squares[1]) / width + EPS)
    scale = math.log2(math.e) / math.sqrt(HD)

    def send_heads(which, source):
        def step(hop, carry):
            other = lax.rem(seq + hop, members)
            columns = pl.ds(pl.multiple_of(other * HD, HD), HD)
            pltpu.make_async_remote_copy(
                src_ref=source.at[:, columns],
                dst_ref=heads.at[which, my_rows],
                send_sem=head_send.at[which],
                recv_sem=head_recv.at[which],
                device_id=(span, other, mp),
                device_id_type=MESH,
            ).start()
            return carry

        lax.fori_loop(1, members, step, 0)

    for which, gain in enumerate((q_gain, k_gain)):
        at = which * (HD // 2)
        factor = factors[:, at : at + 1] * (scale if which == 0 else 1.0)
        normed[which] = (
            raw[which].astype(jnp.float32) * factor * gain[...][None, :]
        ).astype(jnp.bfloat16)
        own = pltpu.make_async_copy(
            normed.at[which, :, my_columns], heads.at[which, my_rows], local_sem.at[3 + which]
        )
        own.start()
        owns.append(own)
        send_heads(which, normed.at[which])
    send_heads(2, value.at[0])

    owns[0].wait()
    owns[1].wait()
    for dz in range(ring_z):
        count = (ring_x - 1 if dz == 0 else ring_x) * tokens
        arrived = cached.at[0, :, pl.ds(0, count)]
        pltpu.make_async_copy(arrived, arrived, cache_recv.at[dz]).wait()
        part = cached.at[0, :, group_rows(dz)]
        for dy in (1, 3, 2):
            pltpu.make_async_remote_copy(
                src_ref=part,
                dst_ref=cached.at[2 * (chips_y - dy), :, group_rows(dz)],
                send_sem=y_send.at[dy - 1],
                recv_sem=y_recv.at[chips_y - dy - 1, dz],
                device_id=(lax.rem(y + dy, chips_y) * 2 + core, seq, mp),
                device_id_type=MESH,
            ).start()
        pltpu.make_async_remote_copy(
            src_ref=part,
            dst_ref=cached.at[1, :, group_rows(dz)],
            send_sem=core_send.at[0],
            recv_sem=core_recv.at[0],
            device_id=partner,
            device_id_type=MESH,
        ).start()

    def attend(rows, keys, values, hide_max, hide_sum):
        scores = lax.dot_general(
            heads[0, rows],
            keys,
            (((1,), (1,)), ((), ())),
            preferred_element_type=jnp.float32,
        )
        before = top[rows]
        now = jnp.maximum(before, jnp.max(scores, axis=-1, keepdims=True) - hide_max)
        shift = (now + hide_sum)[:, :1]
        weights = jnp.exp2(scores - shift)
        shrink = jnp.exp2(before - now)
        top[rows] = now
        mass[rows] = mass[rows] * shrink + jnp.sum(weights, axis=-1, keepdims=True)
        total[rows] = total[rows] * shrink + jnp.dot(
            weights.astype(jnp.bfloat16), values, preferred_element_type=jnp.float32
        )

    def block(slot, dy, dc):
        other = lax.rem(y + dy, chips_y) * 2 + lax.rem(core + dc, 2)
        mine, theirs = span_order[span], span_order[other]
        seen = jnp.where(theirs < mine, context_mask[mine, theirs], 0)
        hide_max = jnp.where(seen > 0, 0.0, OUT_OF_MAX).astype(jnp.float32)
        hide_sum = jnp.where(seen > 0, 0.0, OUT_OF_SUM).astype(jnp.float32)

        def part(index, carry):
            rows = pl.ds(pl.multiple_of(index * group, group), group)
            attend(rows, cached[slot, 0], cached[slot, 1], hide_max, hide_sum)
            return carry

        lax.fori_loop(0, ring_z, part, 0)

    top[...] = jnp.full_like(top, -3e38)
    mass[...] = jnp.zeros_like(mass)
    total[...] = jnp.zeros_like(total)
    arrived = heads.at[0, pl.ds(0, length - tokens)]
    owns[3].wait()
    pltpu.make_async_copy(arrived, arrived, head_recv.at[0]).wait()
    whole = cached.at[1]
    pltpu.make_async_copy(whole, whole, core_recv.at[0]).wait()
    block(1, 0, 1)
    for dy in (1, 3, 2):
        for dz in range(ring_z):
            part = cached.at[2 * dy, :, group_rows(dz)]
            pltpu.make_async_copy(part, part, y_recv.at[dy - 1, dz]).wait()
            pltpu.make_async_remote_copy(
                src_ref=part,
                dst_ref=cached.at[2 * dy + 1, :, group_rows(dz)],
                send_sem=core_send.at[dy],
                recv_sem=core_recv.at[dy],
                device_id=partner,
                device_id_type=MESH,
            ).start()
        block(2 * dy, dy, 0)
        whole = cached.at[2 * dy + 1]
        pltpu.make_async_copy(whole, whole, core_recv.at[dy]).wait()
        block(2 * dy + 1, dy, 1)

    loads[2].wait()
    for which in (1, 2):
        owns[2 if which == 2 else 4].wait()
        arrived = heads.at[which, pl.ds(0, length - tokens)]
        pltpu.make_async_copy(arrived, arrived, head_recv.at[which]).wait()
    steps = lax.broadcasted_iota(jnp.int32, gates.shape, 0)
    gate = jnp.sum(jnp.where(steps == noise_step[span], gates[...], 0.0), axis=0, keepdims=True)
    for dz in (2, 1, 3, 0):
        to_z = lax.rem(z + dz, ring_z)
        rows = pl.ds(pl.multiple_of(to_z * group, group), group)
        attend(rows, heads[1], heads[2], 0.0, 0.0)
        attended = total[rows] / mass[rows]
        factor = lax.rsqrt(jnp.mean(attended * attended, axis=-1, keepdims=True) + EPS)
        done[rows] = (attended * factor * gate).astype(jnp.bfloat16)

        def send_out(dx, carry, dz=dz):
            other = peer(dz, dx)
            pltpu.make_async_remote_copy(
                src_ref=done.at[pl.ds(pl.multiple_of(other * tokens, tokens), tokens)],
                dst_ref=out.at[0, :, my_columns],
                send_sem=out_send,
                recv_sem=out_recv,
                device_id=(span, other, mp),
                device_id_type=MESH,
            ).start()
            return carry

        lax.fori_loop(1 if dz == 0 else 0, ring_x, send_out, 0)
    keep = pltpu.make_async_copy(done.at[my_rows], out.at[0, :, my_columns], local_sem.at[5])
    keep.start()
    keep.wait()

    sent = heads.at[0, pl.ds(0, length - tokens)]
    for sem in (cache_send.at[0], cache_send.at[1], head_send.at[0], head_send.at[1], head_send.at[2]):
        pltpu.make_async_copy(sent, sent, sem).wait()
    whole = cached.at[0]
    for dy in range(1, chips_y):
        pltpu.make_async_copy(whole, whole, y_send.at[dy - 1]).wait()
    for dy in range(chips_y):
        pltpu.make_async_copy(whole, whole, core_send.at[dy]).wait()
    pltpu.make_async_copy(sent, sent, out_send).wait()
    pltpu.make_async_copy(sent, sent, out_recv).wait()


def shards(
    query,
    key,
    value,
    cache_key,
    cache_value,
    q_gain,
    k_gain,
    gate_table,
    span_order,
    noise_step,
    context_mask,
):
    spans, members = lax.axis_size("span"), lax.axis_size("seq")
    chips_y = spans // 2
    ring_x = 4
    ring_z = members // ring_x
    tokens, columns = query.shape[1:]
    length = tokens * members
    dma = pltpu.SemaphoreType.DMA
    anywhere = pl.BlockSpec(memory_space=pl.ANY)
    in_vmem = pl.BlockSpec(memory_space=pltpu.VMEM)
    in_smem = pl.BlockSpec(memory_space=pltpu.SMEM)
    bf16, f32 = jnp.bfloat16, jnp.float32
    return pl.pallas_call(
        functools.partial(exchange_and_attend, chips_y, ring_z, ring_x),
        out_shape=jax.ShapeDtypeStruct(query.shape, bf16),
        in_specs=[anywhere] * 5 + [in_vmem] * 2 + [anywhere] + [in_smem] * 3,
        out_specs=in_vmem,
        scratch_shapes=[
            pltpu.VMEM((2, tokens, columns), bf16),
            pltpu.VMEM((2, tokens, columns), bf16),
            pltpu.VMEM((2, tokens, HD), f32),
            pltpu.VMEM((gate_table.shape[0], HD), f32),
            pltpu.VMEM((3, length, HD), bf16),
            pltpu.VMEM((spans, 2, length, HD), bf16),
            pltpu.VMEM((length, HD), f32),
            pltpu.VMEM((length, HD), f32),
            pltpu.VMEM((length, HD), f32),
            pltpu.VMEM((length, HD), bf16),
            dma((3,)),
            dma((6,)),
            dma,
            dma,
            dma((2,)),
            dma((ring_z,)),
            dma((3,)),
            dma((3,)),
            dma((chips_y - 1,)),
            dma((chips_y - 1, ring_z)),
            dma((chips_y,)),
            dma((chips_y,)),
            dma,
            dma,
        ],
        compiler_params=pltpu.CompilerParams(
            collective_id=0, has_side_effects=True, vmem_limit_bytes=48 << 20
        ),
        name="exchange_and_attend",
    )(
        query,
        key,
        value,
        cache_key,
        cache_value,
        q_gain,
        k_gain,
        gate_table,
        span_order,
        noise_step,
        context_mask,
    )


def solution(mesh):
    placed = (
        P("span", "seq", "mp"),
        P("span", "seq", "mp"),
        P("span", "seq", "mp"),
        P("span", "seq", "mp"),
        P("span", "seq", "mp"),
        P("mp"),
        P("mp"),
        P(None, "mp"),
        P(),
        P(),
        P(),
    )
    return jax.shard_map(
        shards, mesh=mesh, in_specs=placed, out_specs=P("span", "seq", "mp"), check_vma=False
    )
```

```python
import functools
import math

import jax
import jax.numpy as jnp
from jax import lax
from jax.experimental import pallas as pl
from jax.experimental.pallas import tpu as pltpu
from jax.sharding import PartitionSpec as P

MESH = pl.DeviceIdType.MESH
HEADS = 32
HD = 128
EPS = 1e-6
Z_ORDER = (0, 1, 3, 2)
HALVES = 2
EARLY = 3
BLOCKS = ((0, 1), (1, 0), (3, 0), (1, 1), (3, 1), (2, 0), (2, 1))
OWN = len(BLOCKS)
STAGED = OWN + 1
NEAR = (2, 1)
FAR = 5
ONES = 16
WAITS = (
    (1, (("core", 1, 0),)),
    (2, (("core", 2, 0), ("staged", 3))),
    (3, (("near", 2), ("far", 1))),
    (4, (("core", 3, 0), ("far", 2))),
    (5, (("near", 3),)),
    (6, (("core", 0, 1),)),
    (8, (("far", 3),)),
    (9, (("core", 1, 1),)),
    (10, (("core", 2, 1),)),
    (12, (("core", 3, 1),)),
)
OUT_OF_MAX = 1e30
OUT_OF_SUM = 3e30


def exchange_and_attend(
    chips_y,
    ring_z,
    ring_x,
    query,
    key,
    value,
    cache_key,
    cache_value,
    q_gain,
    k_gain,
    gate_table,
    span_order,
    noise_step,
    context_mask,
    result,
    gains,
    order,
    noise,
    mask,
    raw,
    normed,
    squares,
    gates,
    hide,
    queries,
    queries_t,
    blocks,
    scores,
    own_scores,
    total,
    top,
    mass,
    done,
    load_sem,
    local_sem,
    mp_send,
    mp_recv,
    cache_send,
    cache_recv,
    head_send,
    head_recv,
    near_send,
    near_recv,
    far_send,
    far_recv,
    core_send,
    core_recv,
    out_send,
    out_recv,
):
    out = result
    span = lax.axis_index("span")
    seq = lax.axis_index("seq")
    mp = lax.axis_index("mp")
    y, core = span // 2, span % 2
    z, x = seq // ring_x, seq % ring_x
    members = ring_z * ring_x
    tokens = raw.shape[1]
    group = ring_x * tokens
    length = members * tokens
    width = HEADS * HD
    partner = (y * 2 + (1 - core), seq, mp)
    my_rows = pl.ds(pl.multiple_of(seq * tokens, tokens), tokens)
    my_columns = pl.ds(pl.multiple_of(seq * HD, HD), HD)

    def peer(dz, dx):
        return lax.rem(z + dz, ring_z) * ring_x + lax.rem(x + dx, ring_x)

    def stage_rows(stage):
        return pl.ds(stage * group, group)

    def landing(stage):
        return pl.ds(pl.multiple_of(stage * group + x * tokens, tokens), tokens)

    barrier = pltpu.get_barrier_semaphore()

    def greet(step, carry):
        other = lax.rem(seq + step, members)
        pl.semaphore_signal(barrier, inc=1, device_id=(span, other, mp), device_id_type=MESH)
        return carry

    lax.fori_loop(1, members, greet, 0)
    for dy in range(1, chips_y):
        pl.semaphore_signal(
            barrier,
            inc=1,
            device_id=(lax.rem(y + dy, chips_y) * 2 + core, seq, mp),
            device_id_type=MESH,
        )
    pl.semaphore_signal(barrier, inc=1, device_id=partner, device_id_type=MESH)
    pl.semaphore_signal(barrier, inc=1, device_id=(span, seq, 1 - mp), device_id_type=MESH)

    loads = [
        pltpu.make_async_copy(source, target, load_sem.at[index])
        for index, (source, target) in enumerate(
            (
                (query.at[0], raw.at[0]),
                (key.at[0], raw.at[1]),
                (q_gain, gains.at[0]),
                (k_gain, gains.at[1]),
                (gate_table.at[:, my_columns], gates),
                (span_order, order),
                (noise_step, noise),
                (context_mask, mask),
                (cache_key.at[0], raw.at[2]),
                (cache_value.at[0], raw.at[3]),
                (value.at[0], raw.at[4]),
            )
        )
    ]
    for load in loads:
        load.start()
    loads[0].wait()
    loads[1].wait()
    lane = lax.broadcasted_iota(jnp.int32, (tokens, HD), 1)

    def row_squares(which):
        wide = raw[which].astype(jnp.float32)
        return jnp.sum(wide * wide, axis=-1, keepdims=True)

    squares[0] = jnp.where(lane < HD // 2, row_squares(0), row_squares(1))
    for load in loads[8:]:
        load.wait()
    owns = [
        pltpu.make_async_copy(
            raw.at[2, :, my_columns], blocks.at[STAGED, 0, landing(0)], local_sem.at[0]
        ),
        pltpu.make_async_copy(
            raw.at[3, :, my_columns], blocks.at[STAGED, 1, landing(0)], local_sem.at[1]
        ),
        pltpu.make_async_copy(raw.at[4, :, my_columns], blocks.at[OWN, 1, landing(0)], local_sem.at[2]),
    ]
    for own in owns:
        own.start()
    pl.semaphore_wait(barrier, members - 1 + chips_y - 1 + 2)
    swap = pltpu.make_async_remote_copy(
        src_ref=squares.at[0],
        dst_ref=squares.at[1],
        send_sem=mp_send,
        recv_sem=mp_recv,
        device_id=(span, seq, 1 - mp),
        device_id_type=MESH,
    )
    swap.start()

    def send_caches(stage):
        dz = Z_ORDER[stage]

        def send(dx, carry):
            other = peer(dz, dx)
            columns = pl.ds(pl.multiple_of(other * HD, HD), HD)
            for which in range(2):
                pltpu.make_async_remote_copy(
                    src_ref=raw.at[2 + which, :, columns],
                    dst_ref=blocks.at[STAGED, which, landing(stage)],
                    send_sem=cache_send.at[which],
                    recv_sem=cache_recv.at[stage],
                    device_id=(span, other, mp),
                    device_id_type=MESH,
                ).start()
            return carry

        lax.fori_loop(1 if dz == 0 else 0, ring_x, send, 0)

    for stage in range(EARLY):
        send_caches(stage)

    def to_core(source, target, stage, index):
        pltpu.make_async_remote_copy(
            src_ref=blocks.at[source, :, stage_rows(stage)],
            dst_ref=blocks.at[target, :, stage_rows(stage)],
            send_sem=core_send.at[index],
            recv_sem=core_recv.at[index, stage * HALVES // ring_z],
            device_id=partner,
            device_id_type=MESH,
        ).start()

    def along_y(way):
        return (lax.rem(y + (1, chips_y - 1)[way], chips_y) * 2 + core, seq, mp)

    def pass_near(stage):
        for way, place in enumerate(NEAR):
            part = blocks.at[place, :, stage_rows(stage)]
            pltpu.make_async_copy(part, part, near_recv.at[way, stage]).wait()
            pltpu.make_async_remote_copy(
                src_ref=blocks.at[place, way, stage_rows(stage)],
                dst_ref=blocks.at[FAR, way, stage_rows(stage)],
                send_sem=far_send.at[way],
                recv_sem=far_recv.at[way, stage],
                device_id=along_y(way),
                device_id_type=MESH,
            ).start()
            to_core(place, place + 2, stage, place)

    def pass_far(stage):
        for way in range(2):
            part = blocks.at[FAR, way, stage_rows(stage)]
            pltpu.make_async_copy(part, part, far_recv.at[way, stage]).wait()
        to_core(FAR, FAR + 1, stage, 3)

    def await_core(index, half):
        rows = pl.ds(half * (length // HALVES), length // HALVES)
        part = blocks.at[(0, 3, 4, 6)[index], :, rows]
        pltpu.make_async_copy(part, part, core_recv.at[index, half]).wait()

    owns[0].wait()
    owns[1].wait()
    def pass_staged(stage):
        count = (ring_x - 1 if Z_ORDER[stage] == 0 else ring_x) * tokens
        arrived = blocks.at[STAGED, :, pl.ds(0, count)]
        pltpu.make_async_copy(arrived, arrived, cache_recv.at[stage]).wait()
        for way, place in enumerate(NEAR):
            pltpu.make_async_remote_copy(
                src_ref=blocks.at[STAGED, :, stage_rows(stage)],
                dst_ref=blocks.at[place, :, stage_rows(stage)],
                send_sem=near_send.at[way],
                recv_sem=near_recv.at[way, stage],
                device_id=along_y(way),
                device_id_type=MESH,
            ).start()
        to_core(STAGED, 0, stage, 0)

    pass_staged(0)

    swap.wait()
    loads[2].wait()
    loads[3].wait()
    factors = lax.rsqrt((squares[0] + squares[1]) / width + EPS)
    scale = math.log2(math.e) / math.sqrt(HD)

    def send_heads(which, source):
        for stage, dz in enumerate(Z_ORDER):

            def send(dx, carry, stage=stage, dz=dz):
                other = peer(dz, dx)
                columns = pl.ds(pl.multiple_of(other * HD, HD), HD)
                if which == 0:
                    target = queries.at[my_rows]
                else:
                    target = blocks.at[OWN, which - 1, landing(stage)]
                pltpu.make_async_remote_copy(
                    src_ref=source.at[:, columns],
                    dst_ref=target,
                    send_sem=head_send.at[which],
                    recv_sem=head_recv.at[which],
                    device_id=(span, other, mp),
                    device_id_type=MESH,
                ).start()
                return carry

            lax.fori_loop(1 if dz == 0 else 0, ring_x, send, 0)

    for which in range(2):
        at = which * (HD // 2)
        factor = factors[:, at : at + 1] * (scale if which == 0 else 1.0)
        normed[which] = (
            raw[which].astype(jnp.float32) * factor * gains[which][None, :]
        ).astype(jnp.bfloat16)
        own = pltpu.make_async_copy(
            normed.at[which, :, my_columns],
            queries.at[my_rows] if which == 0 else blocks.at[OWN, 0, landing(0)],
            local_sem.at[3 + which],
        )
        own.start()
        owns.append(own)
        send_heads(which, normed.at[which])
        if which == 0:
            for stage in range(EARLY, ring_z):
                send_caches(stage)
    send_heads(2, raw.at[4])

    pass_staged(1)
    pass_near(0)
    pass_staged(2)
    pass_near(1)
    pass_far(0)

    for load in loads[4:8]:
        load.wait()
    for place, (dy, dc) in enumerate(BLOCKS):
        other = lax.rem(y + dy, chips_y) * 2 + lax.rem(core + dc, 2)
        mine, theirs = order[span], order[other]
        seen = jnp.where(theirs < mine, mask[mine, theirs], 0)
        hide[0, place] = jnp.where(seen > 0, 0.0, OUT_OF_MAX).astype(jnp.float32)
        hide[1, place] = jnp.where(seen > 0, 0.0, OUT_OF_SUM).astype(jnp.float32)

    span_rows = length // HALVES
    count = HALVES * len(BLOCKS)

    def rows_of(half):
        return pl.ds(pl.multiple_of(half * span_rows, span_rows), span_rows)

    def score(index, slot, columns):
        scores[slot, :, columns] = jnp.dot(
            blocks[lax.rem(index, len(BLOCKS)), 0, rows_of(index // len(BLOCKS))],
            queries_t[:, columns],
            preferred_element_type=jnp.float32,
        )

    def with_ones(values):
        return jnp.concatenate([values.T, jnp.ones((ONES, values.shape[0]), jnp.bfloat16)], axis=0)

    def weigh(block, columns, values, hide_max, hide_sum):
        before = top[:, columns]
        now = jnp.maximum(before, jnp.max(block, axis=0, keepdims=True) - hide_max)
        weights = jnp.exp2(block - (now + hide_sum)).astype(jnp.bfloat16)
        shrink = jnp.exp2(before - now)
        sums = jnp.dot(values, weights, preferred_element_type=jnp.float32)
        top[:, columns] = now
        mass[:, columns] = mass[:, columns] * shrink + sums[HD : HD + 1]
        total[:, columns] = total[:, columns] * shrink + sums[:HD]

    def weigh_at(index, slot, columns, values):
        place = lax.rem(index, len(BLOCKS))
        weigh(scores[slot, :, columns], columns, values, hide[0, place], hide[1, place])

    def values_at(index):
        return with_ones(blocks[lax.rem(index, len(BLOCKS)), 1, rows_of(index // len(BLOCKS))])

    top[...] = jnp.full_like(top, -3e38)
    mass[...] = jnp.zeros_like(mass)
    total[...] = jnp.zeros_like(total)
    sent = queries.at[pl.ds(0, length - tokens)]
    owns[3].wait()
    pltpu.make_async_copy(sent, sent, head_recv.at[0]).wait()
    queries_t[...] = queries[...].T
    await_core(0, 0)
    parts = [pl.ds(index * group, group) for index in range(ring_z)]
    for columns in parts:
        score(0, 0, columns)

    passing = {"staged": pass_staged, "near": pass_near, "far": pass_far, "core": await_core}

    def one_step(index, slot):
        for when, todo in WAITS:
            if when % 2 == slot:

                @pl.when(index == when)
                def _(todo=todo):
                    for what, *which in todo:
                        passing[what](*which)

        values = values_at(index)
        for columns in parts:
            score(index + 1, 1 - slot, columns)
            weigh_at(index, slot, columns, values)

    def two_steps(pair, carry):
        one_step(2 * pair, 0)
        one_step(2 * pair + 1, 1)
        return carry

    lax.fori_loop(0, count // 2 - 1, two_steps, 0)
    one_step(jnp.int32(count - 2), 0)
    owns[4].wait()
    pltpu.make_async_copy(sent, sent, head_recv.at[1]).wait()
    values = values_at(jnp.int32(count - 1))
    for columns in parts:
        own_scores[:, columns] = jnp.dot(
            blocks[OWN, 0], queries_t[:, columns], preferred_element_type=jnp.float32
        )
        weigh_at(jnp.int32(count - 1), 1, columns, values)

    owns[2].wait()
    pltpu.make_async_copy(sent, sent, head_recv.at[2]).wait()
    steps = lax.broadcasted_iota(jnp.int32, gates.shape, 0)
    gate = jnp.sum(jnp.where(steps == noise[span], gates[...], 0.0), axis=0, keepdims=True)
    values = with_ones(blocks[OWN, 1])
    for dz in (2, 1, 3, 0):
        rows = pl.ds(pl.multiple_of(lax.rem(z + dz, ring_z) * group, group), group)
        weigh(own_scores[:, rows], rows, values, 0.0, 0.0)
        attended = total[:, rows] / mass[:, rows]
        factor = lax.rsqrt(jnp.mean(attended * attended, axis=0, keepdims=True) + EPS)
        done[rows] = ((attended * factor).T * gate).astype(jnp.bfloat16)

        def send_out(dx, carry, dz=dz):
            other = peer(dz, dx)
            pltpu.make_async_remote_copy(
                src_ref=done.at[pl.ds(pl.multiple_of(other * tokens, tokens), tokens)],
                dst_ref=out.at[0, :, my_columns],
                send_sem=out_send,
                recv_sem=out_recv,
                device_id=(span, other, mp),
                device_id_type=MESH,
            ).start()
            return carry

        lax.fori_loop(1 if dz == 0 else 0, ring_x, send_out, 0)
    keep = pltpu.make_async_copy(done.at[my_rows], out.at[0, :, my_columns], local_sem.at[5])
    keep.start()
    keep.wait()

    for sem in (cache_send.at[0], cache_send.at[1], head_send.at[0], head_send.at[1], head_send.at[2]):
        pltpu.make_async_copy(sent, sent, sem).wait()
    whole = blocks.at[STAGED]
    for way in range(2):
        pltpu.make_async_copy(whole, whole, near_send.at[way]).wait()
        pltpu.make_async_copy(whole.at[0], whole.at[0], far_send.at[way]).wait()
    for index in range(chips_y):
        pltpu.make_async_copy(whole, whole, core_send.at[index]).wait()
    pltpu.make_async_copy(sent, sent, out_send).wait()
    pltpu.make_async_copy(sent, sent, out_recv).wait()


def shards(
    query,
    key,
    value,
    cache_key,
    cache_value,
    q_gain,
    k_gain,
    gate_table,
    span_order,
    noise_step,
    context_mask,
):
    spans, members = lax.axis_size("span"), lax.axis_size("seq")
    chips_y = spans // 2
    ring_x = 4
    ring_z = members // ring_x
    tokens, columns = query.shape[1:]
    length = tokens * members
    dma = pltpu.SemaphoreType.DMA
    in_hbm = pl.BlockSpec(memory_space=pltpu.HBM)
    in_vmem = pl.BlockSpec(memory_space=pltpu.VMEM)
    bf16, f32 = jnp.bfloat16, jnp.float32
    return pl.pallas_call(
        functools.partial(exchange_and_attend, chips_y, ring_z, ring_x),
        out_shape=jax.ShapeDtypeStruct(query.shape, bf16),
        in_specs=[in_hbm] * 11,
        out_specs=in_vmem,
        scratch_shapes=[
            pltpu.VMEM((2, columns), f32),
            pltpu.SMEM(span_order.shape, jnp.int32),
            pltpu.SMEM(noise_step.shape, jnp.int32),
            pltpu.SMEM(context_mask.shape, jnp.int32),
            pltpu.VMEM((5, tokens, columns), bf16),
            pltpu.VMEM((2, tokens, columns), bf16),
            pltpu.VMEM((2, tokens, HD), f32),
            pltpu.VMEM((gate_table.shape[0], HD), f32),
            pltpu.SMEM((2, len(BLOCKS)), f32),
            pltpu.VMEM((length, HD), bf16),
            pltpu.VMEM((HD, length), bf16),
            pltpu.VMEM((len(BLOCKS) + 2, 2, length, HD), bf16),
            pltpu.VMEM((2, length // HALVES, length), f32),
            pltpu.VMEM((length, length), f32),
            pltpu.VMEM((HD, length), f32),
            pltpu.VMEM((1, length), f32),
            pltpu.VMEM((1, length), f32),
            pltpu.VMEM((length, HD), bf16),
            dma((11,)),
            dma((6,)),
            dma,
            dma,
            dma((2,)),
            dma((ring_z,)),
            dma((3,)),
            dma((3,)),
            dma((2,)),
            dma((2, ring_z)),
            dma((2,)),
            dma((2, ring_z)),
            dma((chips_y,)),
            dma((chips_y, HALVES)),
            dma,
            dma,
        ],
        compiler_params=pltpu.CompilerParams(
            collective_id=0, has_side_effects=True, vmem_limit_bytes=63 << 20
        ),
        name="exchange_and_attend",
    )(
        query,
        key,
        value,
        cache_key,
        cache_value,
        q_gain,
        k_gain,
        gate_table,
        span_order,
        noise_step,
        context_mask,
    )


def solution(mesh):
    placed = (
        P("span", "seq", "mp"),
        P("span", "seq", "mp"),
        P("span", "seq", "mp"),
        P("span", "seq", "mp"),
        P("span", "seq", "mp"),
        P("mp"),
        P("mp"),
        P(None, "mp"),
        P(),
        P(),
        P(),
    )
    return jax.shard_map(
        shards, mesh=mesh, in_specs=placed, out_specs=P("span", "seq", "mp"), check_vma=False
    )
```

```python
import functools
import math

import jax
import jax.numpy as jnp
from jax import lax
from jax.experimental import pallas as pl
from jax.experimental.pallas import tpu as pltpu
from jax.sharding import PartitionSpec as P

MESH = pl.DeviceIdType.MESH
HEADS = 32
HD = 128
EPS = 1e-6
Z_ORDER = (0, 1, 3, 2)
HALVES = 2
BLOCKS = ((0, 1), (1, 0), (3, 0), (1, 1), (3, 1), (2, 0), (2, 1))
OWN = len(BLOCKS)
STAGED = OWN + 1
NEAR = (2, 1)
FAR = 5
ONES = 16
WAITS = (
    (1, (("core", 1, 0), ("near", 3))),
    (2, (("core", 2, 0),)),
    (3, (("far", 2),)),
    (4, (("core", 3, 0),)),
    (5, (("far", 3),)),
    (6, (("core", 0, 1),)),
    (9, (("core", 1, 1),)),
    (10, (("core", 2, 1),)),
    (12, (("core", 3, 1),)),
)
OUT_OF_MAX = 1e30
OUT_OF_SUM = 3e30


def exchange_and_attend(
    chips_y,
    ring_z,
    ring_x,
    query,
    key,
    value,
    cache_key,
    cache_value,
    q_gain,
    k_gain,
    gate_table,
    span_order,
    noise_step,
    context_mask,
    out,
    gains,
    order,
    noise,
    mask,
    raw,
    normed,
    squares,
    gates,
    hide,
    queries,
    queries_t,
    blocks,
    scores,
    own_scores,
    total,
    top,
    mass,
    done,
    load_sem,
    local_sem,
    mp_send,
    mp_recv,
    cache_send,
    cache_recv,
    head_send,
    head_recv,
    near_send,
    near_recv,
    far_send,
    far_recv,
    core_send,
    core_recv,
    out_send,
    out_recv,
):
    span = lax.axis_index("span")
    seq = lax.axis_index("seq")
    mp = lax.axis_index("mp")
    y, core = span // 2, span % 2
    z, x = seq // ring_x, seq % ring_x
    members = ring_z * ring_x
    tokens = raw.shape[1]
    group = ring_x * tokens
    length = members * tokens
    width = HEADS * HD
    partner = (y * 2 + (1 - core), seq, mp)
    my_rows = pl.ds(pl.multiple_of(seq * tokens, tokens), tokens)
    my_columns = pl.ds(pl.multiple_of(seq * HD, HD), HD)

    def peer(dz, dx):
        return lax.rem(z + dz, ring_z) * ring_x + lax.rem(x + dx, ring_x)

    def stage_rows(stage):
        return pl.ds(stage * group, group)

    def landing(stage):
        return pl.ds(pl.multiple_of(stage * group + x * tokens, tokens), tokens)

    barrier = pltpu.get_barrier_semaphore()

    def greet(step, carry):
        other = lax.rem(seq + step, members)
        pl.semaphore_signal(barrier, inc=1, device_id=(span, other, mp), device_id_type=MESH)
        return carry

    lax.fori_loop(1, members, greet, 0)
    for dy in range(1, chips_y):
        pl.semaphore_signal(
            barrier,
            inc=1,
            device_id=(lax.rem(y + dy, chips_y) * 2 + core, seq, mp),
            device_id_type=MESH,
        )
    pl.semaphore_signal(barrier, inc=1, device_id=partner, device_id_type=MESH)
    pl.semaphore_signal(barrier, inc=1, device_id=(span, seq, 1 - mp), device_id_type=MESH)

    loads = [
        pltpu.make_async_copy(source, target, load_sem.at[index])
        for index, (source, target) in enumerate(
            (
                (query.at[0], raw.at[0]),
                (key.at[0], raw.at[1]),
                (q_gain, gains.at[0]),
                (k_gain, gains.at[1]),
                (gate_table.at[:, my_columns], gates),
                (span_order, order),
                (noise_step, noise),
                (context_mask, mask),
                (cache_key.at[0], raw.at[2]),
                (cache_value.at[0], raw.at[3]),
                (value.at[0], raw.at[4]),
            )
        )
    ]
    for load in loads:
        load.start()
    loads[0].wait()
    loads[1].wait()
    lane = lax.broadcasted_iota(jnp.int32, (tokens, HD), 1)

    def row_squares(which):
        wide = raw[which].astype(jnp.float32)
        return jnp.sum(wide * wide, axis=-1, keepdims=True)

    squares[0] = jnp.where(lane < HD // 2, row_squares(0), row_squares(1))
    for load in loads[8:]:
        load.wait()
    owns = [
        pltpu.make_async_copy(
            raw.at[2, :, my_columns], blocks.at[STAGED, 0, landing(0)], local_sem.at[0]
        ),
        pltpu.make_async_copy(
            raw.at[3, :, my_columns], blocks.at[STAGED, 1, landing(0)], local_sem.at[1]
        ),
        pltpu.make_async_copy(raw.at[4, :, my_columns], blocks.at[OWN, 1, landing(0)], local_sem.at[2]),
    ]
    for own in owns:
        own.start()
    pl.semaphore_wait(barrier, members - 1 + chips_y - 1 + 2)
    swap = pltpu.make_async_remote_copy(
        src_ref=squares.at[0],
        dst_ref=squares.at[1],
        send_sem=mp_send,
        recv_sem=mp_recv,
        device_id=(span, seq, 1 - mp),
        device_id_type=MESH,
    )
    swap.start()

    def send_caches(stage):
        dz = Z_ORDER[stage]

        def send(dx, carry):
            other = peer(dz, dx)
            columns = pl.ds(pl.multiple_of(other * HD, HD), HD)
            for which in range(2):
                pltpu.make_async_remote_copy(
                    src_ref=raw.at[2 + which, :, columns],
                    dst_ref=blocks.at[STAGED, which, landing(stage)],
                    send_sem=cache_send.at[which],
                    recv_sem=cache_recv.at[stage],
                    device_id=(span, other, mp),
                    device_id_type=MESH,
                ).start()
            return carry

        lax.fori_loop(1 if dz == 0 else 0, ring_x, send, 0)

    for stage in range(ring_z):
        send_caches(stage)

    def to_core(source, target, stage, index):
        pltpu.make_async_remote_copy(
            src_ref=blocks.at[source, :, stage_rows(stage)],
            dst_ref=blocks.at[target, :, stage_rows(stage)],
            send_sem=core_send.at[index],
            recv_sem=core_recv.at[index, stage * HALVES // ring_z],
            device_id=partner,
            device_id_type=MESH,
        ).start()

    def along_y(way):
        return (lax.rem(y + (1, chips_y - 1)[way], chips_y) * 2 + core, seq, mp)

    def pass_near(stage):
        for way, place in enumerate(NEAR):
            part = blocks.at[place, :, stage_rows(stage)]
            pltpu.make_async_copy(part, part, near_recv.at[way, stage]).wait()
            pltpu.make_async_remote_copy(
                src_ref=blocks.at[place, way, stage_rows(stage)],
                dst_ref=blocks.at[FAR, way, stage_rows(stage)],
                send_sem=far_send.at[way],
                recv_sem=far_recv.at[way, stage],
                device_id=along_y(way),
                device_id_type=MESH,
            ).start()
            to_core(place, place + 2, stage, place)

    def pass_far(stage):
        for way in range(2):
            part = blocks.at[FAR, way, stage_rows(stage)]
            pltpu.make_async_copy(part, part, far_recv.at[way, stage]).wait()
        to_core(FAR, FAR + 1, stage, 3)

    def await_core(index, half):
        rows = pl.ds(half * (length // HALVES), length // HALVES)
        part = blocks.at[(0, 3, 4, 6)[index], :, rows]
        pltpu.make_async_copy(part, part, core_recv.at[index, half]).wait()

    owns[0].wait()
    owns[1].wait()
    def pass_staged(stage):
        count = (ring_x - 1 if Z_ORDER[stage] == 0 else ring_x) * tokens
        arrived = blocks.at[STAGED, :, pl.ds(0, count)]
        pltpu.make_async_copy(arrived, arrived, cache_recv.at[stage]).wait()
        for way, place in enumerate(NEAR):
            pltpu.make_async_remote_copy(
                src_ref=blocks.at[STAGED, :, stage_rows(stage)],
                dst_ref=blocks.at[place, :, stage_rows(stage)],
                send_sem=near_send.at[way],
                recv_sem=near_recv.at[way, stage],
                device_id=along_y(way),
                device_id_type=MESH,
            ).start()
        to_core(STAGED, 0, stage, 0)

    pass_staged(0)

    swap.wait()
    loads[2].wait()
    loads[3].wait()
    factors = lax.rsqrt((squares[0] + squares[1]) / width + EPS)
    scale = math.log2(math.e) / math.sqrt(HD)

    def send_heads(which, source):
        for stage, dz in enumerate(Z_ORDER):

            def send(dx, carry, stage=stage, dz=dz):
                other = peer(dz, dx)
                columns = pl.ds(pl.multiple_of(other * HD, HD), HD)
                if which == 0:
                    target = queries.at[my_rows]
                else:
                    target = blocks.at[OWN, which - 1, landing(stage)]
                pltpu.make_async_remote_copy(
                    src_ref=source.at[:, columns],
                    dst_ref=target,
                    send_sem=head_send.at[which],
                    recv_sem=head_recv.at[which],
                    device_id=(span, other, mp),
                    device_id_type=MESH,
                ).start()
                return carry

            lax.fori_loop(1 if dz == 0 else 0, ring_x, send, 0)

    for which in range(2):
        at = which * (HD // 2)
        factor = factors[:, at : at + 1] * (scale if which == 0 else 1.0)
        normed[which] = (
            raw[which].astype(jnp.float32) * factor * gains[which][None, :]
        ).astype(jnp.bfloat16)
        own = pltpu.make_async_copy(
            normed.at[which, :, my_columns],
            queries.at[my_rows] if which == 0 else blocks.at[OWN, 0, landing(0)],
            local_sem.at[3 + which],
        )
        own.start()
        owns.append(own)
        send_heads(which, normed.at[which])
    send_heads(2, raw.at[4])

    pass_staged(1)
    pass_near(0)
    pass_staged(2)
    pass_near(1)
    pass_far(0)
    pass_staged(3)
    pass_near(2)
    pass_far(1)

    for load in loads[4:8]:
        load.wait()
    for place, (dy, dc) in enumerate(BLOCKS):
        other = lax.rem(y + dy, chips_y) * 2 + lax.rem(core + dc, 2)
        mine, theirs = order[span], order[other]
        seen = jnp.where(theirs < mine, mask[mine, theirs], 0)
        hide[0, place] = jnp.where(seen > 0, 0.0, OUT_OF_MAX).astype(jnp.float32)
        hide[1, place] = jnp.where(seen > 0, 0.0, OUT_OF_SUM).astype(jnp.float32)

    span_rows = length // HALVES
    count = HALVES * len(BLOCKS)

    def rows_of(half):
        return pl.ds(pl.multiple_of(half * span_rows, span_rows), span_rows)

    def score(index, slot, columns):
        scores[slot, :, columns] = jnp.dot(
            blocks[lax.rem(index, len(BLOCKS)), 0, rows_of(index // len(BLOCKS))],
            queries_t[:, columns],
            preferred_element_type=jnp.float32,
        )

    def with_ones(values):
        return jnp.concatenate([values.T, jnp.ones((ONES, values.shape[0]), jnp.bfloat16)], axis=0)

    def weigh(block, columns, values, hide_max, hide_sum):
        before = top[:, columns]
        now = jnp.maximum(before, jnp.max(block, axis=0, keepdims=True) - hide_max)
        weights = jnp.exp2(block - (now + hide_sum)).astype(jnp.bfloat16)
        shrink = jnp.exp2(before - now)
        sums = jnp.dot(values, weights, preferred_element_type=jnp.float32)
        top[:, columns] = now
        mass[:, columns] = mass[:, columns] * shrink + sums[HD : HD + 1]
        total[:, columns] = total[:, columns] * shrink + sums[:HD]

    def weigh_at(index, slot, columns, values):
        place = lax.rem(index, len(BLOCKS))
        weigh(scores[slot, :, columns], columns, values, hide[0, place], hide[1, place])

    def values_at(index):
        return with_ones(blocks[lax.rem(index, len(BLOCKS)), 1, rows_of(index // len(BLOCKS))])

    top[...] = jnp.full_like(top, -3e38)
    mass[...] = jnp.zeros_like(mass)
    total[...] = jnp.zeros_like(total)
    sent = queries.at[pl.ds(0, length - tokens)]
    owns[3].wait()
    pltpu.make_async_copy(sent, sent, head_recv.at[0]).wait()
    queries_t[...] = queries[...].T
    await_core(0, 0)
    parts = [pl.ds(index * group, group) for index in range(ring_z)]
    for columns in parts:
        score(0, 0, columns)

    passing = {"staged": pass_staged, "near": pass_near, "far": pass_far, "core": await_core}

    def one_step(index, slot):
        for when, todo in WAITS:
            if when % 2 == slot:

                @pl.when(index == when)
                def _(todo=todo):
                    for what, *which in todo:
                        passing[what](*which)

        values = values_at(index)
        for columns in parts:
            score(index + 1, 1 - slot, columns)
            weigh_at(index, slot, columns, values)

    def two_steps(pair, carry):
        one_step(2 * pair, 0)
        one_step(2 * pair + 1, 1)
        return carry

    lax.fori_loop(0, count // 2 - 1, two_steps, 0)
    one_step(jnp.int32(count - 2), 0)
    owns[4].wait()
    pltpu.make_async_copy(sent, sent, head_recv.at[1]).wait()
    values = values_at(jnp.int32(count - 1))
    for columns in parts:
        own_scores[:, columns] = jnp.dot(
            blocks[OWN, 0], queries_t[:, columns], preferred_element_type=jnp.float32
        )
        weigh_at(jnp.int32(count - 1), 1, columns, values)

    owns[2].wait()
    pltpu.make_async_copy(sent, sent, head_recv.at[2]).wait()
    steps = lax.broadcasted_iota(jnp.int32, gates.shape, 0)
    gate = jnp.sum(jnp.where(steps == noise[span], gates[...], 0.0), axis=0, keepdims=True)
    values = with_ones(blocks[OWN, 1])
    for dz in (2, 1, 3, 0):
        rows = pl.ds(pl.multiple_of(lax.rem(z + dz, ring_z) * group, group), group)
        weigh(own_scores[:, rows], rows, values, 0.0, 0.0)
        attended = total[:, rows] / mass[:, rows]
        factor = lax.rsqrt(jnp.mean(attended * attended, axis=0, keepdims=True) + EPS)
        done[rows] = ((attended * factor).T * gate).astype(jnp.bfloat16)

        def send_out(dx, carry, dz=dz):
            other = peer(dz, dx)
            pltpu.make_async_remote_copy(
                src_ref=done.at[pl.ds(pl.multiple_of(other * tokens, tokens), tokens)],
                dst_ref=out.at[0, :, my_columns],
                send_sem=out_send,
                recv_sem=out_recv,
                device_id=(span, other, mp),
                device_id_type=MESH,
            ).start()
            return carry

        lax.fori_loop(1 if dz == 0 else 0, ring_x, send_out, 0)
    keep = pltpu.make_async_copy(done.at[my_rows], out.at[0, :, my_columns], local_sem.at[5])
    keep.start()
    keep.wait()

    for sem in (cache_send.at[0], cache_send.at[1], head_send.at[0], head_send.at[1], head_send.at[2]):
        pltpu.make_async_copy(sent, sent, sem).wait()
    whole = blocks.at[STAGED]
    for way in range(2):
        pltpu.make_async_copy(whole, whole, near_send.at[way]).wait()
        pltpu.make_async_copy(whole.at[0], whole.at[0], far_send.at[way]).wait()
    for index in range(chips_y):
        pltpu.make_async_copy(whole, whole, core_send.at[index]).wait()
    pltpu.make_async_copy(sent, sent, out_send).wait()
    pltpu.make_async_copy(sent, sent, out_recv).wait()


def shards(
    query,
    key,
    value,
    cache_key,
    cache_value,
    q_gain,
    k_gain,
    gate_table,
    span_order,
    noise_step,
    context_mask,
):
    spans, members = lax.axis_size("span"), lax.axis_size("seq")
    chips_y = spans // 2
    ring_x = 4
    ring_z = members // ring_x
    tokens, columns = query.shape[1:]
    length = tokens * members
    dma = pltpu.SemaphoreType.DMA
    in_hbm = pl.BlockSpec(memory_space=pltpu.HBM)
    bf16, f32 = jnp.bfloat16, jnp.float32
    return pl.pallas_call(
        functools.partial(exchange_and_attend, chips_y, ring_z, ring_x),
        out_shape=jax.ShapeDtypeStruct(query.shape, bf16),
        in_specs=[in_hbm] * 11,
        out_specs=in_hbm,
        scratch_shapes=[
            pltpu.VMEM((2, columns), f32),
            pltpu.SMEM(span_order.shape, jnp.int32),
            pltpu.SMEM(noise_step.shape, jnp.int32),
            pltpu.SMEM(context_mask.shape, jnp.int32),
            pltpu.VMEM((5, tokens, columns), bf16),
            pltpu.VMEM((2, tokens, columns), bf16),
            pltpu.VMEM((2, tokens, HD), f32),
            pltpu.VMEM((gate_table.shape[0], HD), f32),
            pltpu.SMEM((2, len(BLOCKS)), f32),
            pltpu.VMEM((length, HD), bf16),
            pltpu.VMEM((HD, length), bf16),
            pltpu.VMEM((len(BLOCKS) + 2, 2, length, HD), bf16),
            pltpu.VMEM((2, length // HALVES, length), f32),
            pltpu.VMEM((length, length), f32),
            pltpu.VMEM((HD, length), f32),
            pltpu.VMEM((1, length), f32),
            pltpu.VMEM((1, length), f32),
            pltpu.VMEM((length, HD), bf16),
            dma((11,)),
            dma((6,)),
            dma,
            dma,
            dma((2,)),
            dma((ring_z,)),
            dma((3,)),
            dma((3,)),
            dma((2,)),
            dma((2, ring_z)),
            dma((2,)),
            dma((2, ring_z)),
            dma((chips_y,)),
            dma((chips_y, HALVES)),
            dma,
            dma,
        ],
        compiler_params=pltpu.CompilerParams(
            collective_id=0, has_side_effects=True, vmem_limit_bytes=63 << 20
        ),
        name="exchange_and_attend",
    )(
        query,
        key,
        value,
        cache_key,
        cache_value,
        q_gain,
        k_gain,
        gate_table,
        span_order,
        noise_step,
        context_mask,
    )


def solution(mesh):
    placed = (
        P("span", "seq", "mp"),
        P("span", "seq", "mp"),
        P("span", "seq", "mp"),
        P("span", "seq", "mp"),
        P("span", "seq", "mp"),
        P("mp"),
        P("mp"),
        P(None, "mp"),
        P(),
        P(),
        P(),
    )
    return jax.shard_map(
        shards, mesh=mesh, in_specs=placed, out_specs=P("span", "seq", "mp"), check_vma=False
    )
```

```python
import functools
import math

import jax
import jax.numpy as jnp
from jax import lax
from jax.experimental import pallas as pl
from jax.experimental.pallas import tpu as pltpu
from jax.sharding import PartitionSpec as P

MESH = pl.DeviceIdType.MESH
HEADS = 32
HD = 128
EPS = 1e-6
Z_ORDER = (0, 1, 3, 2)
HALVES = 2
BLOCKS = ((0, 1), (1, 0), (3, 0), (1, 1), (3, 1), (2, 0), (2, 1))
OWN = len(BLOCKS)
STAGED = OWN + 1
NEAR = (2, 1)
FAR = 5
ONES = 16
WAITS = (
    (1, (("core", 1, 0), ("near", 3))),
    (2, (("core", 2, 0),)),
    (3, (("far", 2),)),
    (4, (("core", 3, 0),)),
    (5, (("far", 3),)),
    (6, (("core", 0, 1),)),
    (9, (("core", 1, 1),)),
    (10, (("core", 2, 1),)),
    (12, (("core", 3, 1),)),
)
OUT_OF_MAX = 1e30
OUT_OF_SUM = 3e30


def exchange_and_attend(
    chips_y,
    ring_z,
    ring_x,
    query,
    key,
    value,
    cache_key,
    cache_value,
    q_gain,
    k_gain,
    gate_table,
    span_order,
    noise_step,
    context_mask,
    out,
    gains,
    order,
    noise,
    mask,
    raw,
    normed,
    squares,
    gates,
    hide,
    queries,
    queries_t,
    blocks,
    scores,
    own_scores,
    total,
    top,
    mass,
    done,
    load_sem,
    local_sem,
    mp_send,
    mp_recv,
    cache_send,
    cache_recv,
    head_send,
    head_recv,
    near_send,
    near_recv,
    far_send,
    far_recv,
    core_send,
    core_recv,
    out_send,
    out_recv,
):
    span = lax.axis_index("span")
    seq = lax.axis_index("seq")
    mp = lax.axis_index("mp")
    y, core = span // 2, span % 2
    z, x = seq // ring_x, seq % ring_x
    members = ring_z * ring_x
    tokens = raw.shape[1]
    group = ring_x * tokens
    length = members * tokens
    width = HEADS * HD
    partner = (y * 2 + (1 - core), seq, mp)
    my_rows = pl.ds(pl.multiple_of(seq * tokens, tokens), tokens)
    my_columns = pl.ds(pl.multiple_of(seq * HD, HD), HD)

    def peer(dz, dx):
        return lax.rem(z + dz, ring_z) * ring_x + lax.rem(x + dx, ring_x)

    def stage_rows(stage):
        return pl.ds(stage * group, group)

    def landing(stage):
        return pl.ds(pl.multiple_of(stage * group + x * tokens, tokens), tokens)

    barrier = pltpu.get_barrier_semaphore()

    def greet(step, carry):
        other = lax.rem(seq + step, members)
        pl.semaphore_signal(barrier, inc=1, device_id=(span, other, mp), device_id_type=MESH)
        return carry

    lax.fori_loop(1, members, greet, 0)
    for dy in range(1, chips_y):
        pl.semaphore_signal(
            barrier,
            inc=1,
            device_id=(lax.rem(y + dy, chips_y) * 2 + core, seq, mp),
            device_id_type=MESH,
        )
    pl.semaphore_signal(barrier, inc=1, device_id=partner, device_id_type=MESH)
    pl.semaphore_signal(barrier, inc=1, device_id=(span, seq, 1 - mp), device_id_type=MESH)

    loads = [
        pltpu.make_async_copy(source, target, load_sem.at[index])
        for index, (source, target) in enumerate(
            (
                (query.at[0], raw.at[0]),
                (key.at[0], raw.at[1]),
                (q_gain, gains.at[0]),
                (k_gain, gains.at[1]),
                (gate_table.at[:, my_columns], gates),
                (span_order, order),
                (noise_step, noise),
                (context_mask, mask),
            )
        )
    ]
    for load in loads:
        load.start()
    loads[0].wait()
    loads[1].wait()
    lane = lax.broadcasted_iota(jnp.int32, (tokens, HD), 1)

    def row_squares(which):
        wide = raw[which].astype(jnp.float32)
        return jnp.sum(wide * wide, axis=-1, keepdims=True)

    squares[0] = jnp.where(lane < HD // 2, row_squares(0), row_squares(1))
    owns = [
        pltpu.make_async_copy(
            cache_key.at[0, :, my_columns], blocks.at[STAGED, 0, landing(0)], local_sem.at[0]
        ),
        pltpu.make_async_copy(
            cache_value.at[0, :, my_columns], blocks.at[STAGED, 1, landing(0)], local_sem.at[1]
        ),
        pltpu.make_async_copy(value.at[0, :, my_columns], blocks.at[OWN, 1, landing(0)], local_sem.at[2]),
    ]
    for own in owns:
        own.start()
    pl.semaphore_wait(barrier, members - 1 + chips_y - 1 + 2)
    swap = pltpu.make_async_remote_copy(
        src_ref=squares.at[0],
        dst_ref=squares.at[1],
        send_sem=mp_send,
        recv_sem=mp_recv,
        device_id=(span, seq, 1 - mp),
        device_id_type=MESH,
    )
    swap.start()

    def send_caches(stage):
        dz = Z_ORDER[stage]

        def send(dx, carry):
            other = peer(dz, dx)
            columns = pl.ds(pl.multiple_of(other * HD, HD), HD)
            for which in range(2):
                pltpu.make_async_remote_copy(
                    src_ref=(cache_key, cache_value)[which].at[0, :, columns],
                    dst_ref=blocks.at[STAGED, which, landing(stage)],
                    send_sem=cache_send.at[which],
                    recv_sem=cache_recv.at[stage],
                    device_id=(span, other, mp),
                    device_id_type=MESH,
                ).start()
            return carry

        lax.fori_loop(1 if dz == 0 else 0, ring_x, send, 0)

    for stage in range(ring_z):
        send_caches(stage)

    def to_core(source, target, stage, index):
        pltpu.make_async_remote_copy(
            src_ref=blocks.at[source, :, stage_rows(stage)],
            dst_ref=blocks.at[target, :, stage_rows(stage)],
            send_sem=core_send.at[index],
            recv_sem=core_recv.at[index, stage * HALVES // ring_z],
            device_id=partner,
            device_id_type=MESH,
        ).start()

    def along_y(way):
        return (lax.rem(y + (1, chips_y - 1)[way], chips_y) * 2 + core, seq, mp)

    def pass_near(stage):
        for way, place in enumerate(NEAR):
            part = blocks.at[place, :, stage_rows(stage)]
            pltpu.make_async_copy(part, part, near_recv.at[way, stage]).wait()
            pltpu.make_async_remote_copy(
                src_ref=blocks.at[place, way, stage_rows(stage)],
                dst_ref=blocks.at[FAR, way, stage_rows(stage)],
                send_sem=far_send.at[way],
                recv_sem=far_recv.at[way, stage],
                device_id=along_y(way),
                device_id_type=MESH,
            ).start()
            to_core(place, place + 2, stage, place)

    def pass_far(stage):
        for way in range(2):
            part = blocks.at[FAR, way, stage_rows(stage)]
            pltpu.make_async_copy(part, part, far_recv.at[way, stage]).wait()
        to_core(FAR, FAR + 1, stage, 3)

    def await_core(index, half):
        rows = pl.ds(half * (length // HALVES), length // HALVES)
        part = blocks.at[(0, 3, 4, 6)[index], :, rows]
        pltpu.make_async_copy(part, part, core_recv.at[index, half]).wait()

    owns[0].wait()
    owns[1].wait()
    def pass_staged(stage):
        count = (ring_x - 1 if Z_ORDER[stage] == 0 else ring_x) * tokens
        arrived = blocks.at[STAGED, :, pl.ds(0, count)]
        pltpu.make_async_copy(arrived, arrived, cache_recv.at[stage]).wait()
        for way, place in enumerate(NEAR):
            pltpu.make_async_remote_copy(
                src_ref=blocks.at[STAGED, :, stage_rows(stage)],
                dst_ref=blocks.at[place, :, stage_rows(stage)],
                send_sem=near_send.at[way],
                recv_sem=near_recv.at[way, stage],
                device_id=along_y(way),
                device_id_type=MESH,
            ).start()
        to_core(STAGED, 0, stage, 0)

    pass_staged(0)

    swap.wait()
    loads[2].wait()
    loads[3].wait()
    factors = lax.rsqrt((squares[0] + squares[1]) / width + EPS)
    scale = math.log2(math.e) / math.sqrt(HD)

    def send_heads(which, source):
        for stage, dz in enumerate(Z_ORDER):

            def send(dx, carry, stage=stage, dz=dz):
                other = peer(dz, dx)
                columns = pl.ds(pl.multiple_of(other * HD, HD), HD)
                if which == 0:
                    target = queries.at[my_rows]
                else:
                    target = blocks.at[OWN, which - 1, landing(stage)]
                pltpu.make_async_remote_copy(
                    src_ref=source.at[:, columns],
                    dst_ref=target,
                    send_sem=head_send.at[which],
                    recv_sem=head_recv.at[which],
                    device_id=(span, other, mp),
                    device_id_type=MESH,
                ).start()
                return carry

            lax.fori_loop(1 if dz == 0 else 0, ring_x, send, 0)

    for which in range(2):
        at = which * (HD // 2)
        factor = factors[:, at : at + 1] * (scale if which == 0 else 1.0)
        normed[which] = (
            raw[which].astype(jnp.float32) * factor * gains[which][None, :]
        ).astype(jnp.bfloat16)
        own = pltpu.make_async_copy(
            normed.at[which, :, my_columns],
            queries.at[my_rows] if which == 0 else blocks.at[OWN, 0, landing(0)],
            local_sem.at[3 + which],
        )
        own.start()
        owns.append(own)
        send_heads(which, normed.at[which])
    send_heads(2, value.at[0])

    pass_staged(1)
    pass_near(0)
    pass_staged(2)
    pass_near(1)
    pass_far(0)
    pass_staged(3)
    pass_near(2)
    pass_far(1)

    for load in loads[4:8]:
        load.wait()
    for place, (dy, dc) in enumerate(BLOCKS):
        other = lax.rem(y + dy, chips_y) * 2 + lax.rem(core + dc, 2)
        mine, theirs = order[span], order[other]
        seen = jnp.where(theirs < mine, mask[mine, theirs], 0)
        hide[0, place] = jnp.where(seen > 0, 0.0, OUT_OF_MAX).astype(jnp.float32)
        hide[1, place] = jnp.where(seen > 0, 0.0, OUT_OF_SUM).astype(jnp.float32)

    span_rows = length // HALVES
    count = HALVES * len(BLOCKS)

    def rows_of(half):
        return pl.ds(pl.multiple_of(half * span_rows, span_rows), span_rows)

    def score(index, slot, columns):
        scores[slot, :, columns] = jnp.dot(
            blocks[lax.rem(index, len(BLOCKS)), 0, rows_of(index // len(BLOCKS))],
            queries_t[:, columns],
            preferred_element_type=jnp.float32,
        )

    def with_ones(values):
        return jnp.concatenate([values.T, jnp.ones((ONES, values.shape[0]), jnp.bfloat16)], axis=0)

    def weigh(block, columns, values, hide_max, hide_sum):
        before = top[:, columns]
        now = jnp.maximum(before, jnp.max(block, axis=0, keepdims=True) - hide_max)
        weights = jnp.exp2(block - (now + hide_sum)).astype(jnp.bfloat16)
        shrink = jnp.exp2(before - now)
        sums = jnp.dot(values, weights, preferred_element_type=jnp.float32)
        top[:, columns] = now
        mass[:, columns] = mass[:, columns] * shrink + sums[HD : HD + 1]
        total[:, columns] = total[:, columns] * shrink + sums[:HD]

    def weigh_at(index, slot, columns, values):
        place = lax.rem(index, len(BLOCKS))
        weigh(scores[slot, :, columns], columns, values, hide[0, place], hide[1, place])

    def values_at(index):
        return with_ones(blocks[lax.rem(index, len(BLOCKS)), 1, rows_of(index // len(BLOCKS))])

    top[...] = jnp.full_like(top, -3e38)
    mass[...] = jnp.zeros_like(mass)
    total[...] = jnp.zeros_like(total)
    sent = queries.at[pl.ds(0, length - tokens)]
    owns[3].wait()
    pltpu.make_async_copy(sent, sent, head_recv.at[0]).wait()
    queries_t[...] = queries[...].T
    await_core(0, 0)
    parts = [pl.ds(index * 2 * group, 2 * group) for index in range(ring_z // 2)]
    for columns in parts:
        score(0, 0, columns)

    passing = {"staged": pass_staged, "near": pass_near, "far": pass_far, "core": await_core}

    def one_step(index, slot):
        for when, todo in WAITS:
            if when % 2 == slot:

                @pl.when(index == when)
                def _(todo=todo):
                    for what, *which in todo:
                        passing[what](*which)

        values = values_at(index)
        for columns in parts:
            score(index + 1, 1 - slot, columns)
            weigh_at(index, slot, columns, values)

    def two_steps(pair, carry):
        one_step(2 * pair, 0)
        one_step(2 * pair + 1, 1)
        return carry

    lax.fori_loop(0, count // 2 - 1, two_steps, 0)
    one_step(jnp.int32(count - 2), 0)
    owns[4].wait()
    pltpu.make_async_copy(sent, sent, head_recv.at[1]).wait()
    values = values_at(jnp.int32(count - 1))
    for columns in parts:
        own_scores[:, columns] = jnp.dot(
            blocks[OWN, 0], queries_t[:, columns], preferred_element_type=jnp.float32
        )
        weigh_at(jnp.int32(count - 1), 1, columns, values)

    owns[2].wait()
    pltpu.make_async_copy(sent, sent, head_recv.at[2]).wait()
    steps = lax.broadcasted_iota(jnp.int32, gates.shape, 0)
    gate = jnp.sum(jnp.where(steps == noise[span], gates[...], 0.0), axis=0, keepdims=True)
    values = with_ones(blocks[OWN, 1])
    for dz in (2, 1, 3, 0):
        rows = pl.ds(pl.multiple_of(lax.rem(z + dz, ring_z) * group, group), group)
        weigh(own_scores[:, rows], rows, values, 0.0, 0.0)
        attended = total[:, rows] / mass[:, rows]
        factor = lax.rsqrt(jnp.mean(attended * attended, axis=0, keepdims=True) + EPS)
        done[rows] = ((attended * factor).T * gate).astype(jnp.bfloat16)

        def send_out(dx, carry, dz=dz):
            other = peer(dz, dx)
            pltpu.make_async_remote_copy(
                src_ref=done.at[pl.ds(pl.multiple_of(other * tokens, tokens), tokens)],
                dst_ref=out.at[0, :, my_columns],
                send_sem=out_send,
                recv_sem=out_recv,
                device_id=(span, other, mp),
                device_id_type=MESH,
            ).start()
            return carry

        lax.fori_loop(1 if dz == 0 else 0, ring_x, send_out, 0)
    keep = pltpu.make_async_copy(done.at[my_rows], out.at[0, :, my_columns], local_sem.at[5])
    keep.start()
    keep.wait()

    for sem in (cache_send.at[0], cache_send.at[1], head_send.at[0], head_send.at[1], head_send.at[2]):
        pltpu.make_async_copy(sent, sent, sem).wait()
    whole = blocks.at[STAGED]
    for way in range(2):
        pltpu.make_async_copy(whole, whole, near_send.at[way]).wait()
        pltpu.make_async_copy(whole.at[0], whole.at[0], far_send.at[way]).wait()
    for index in range(chips_y):
        pltpu.make_async_copy(whole, whole, core_send.at[index]).wait()
    pltpu.make_async_copy(sent, sent, out_send).wait()
    pltpu.make_async_copy(sent, sent, out_recv).wait()


def shards(
    query,
    key,
    value,
    cache_key,
    cache_value,
    q_gain,
    k_gain,
    gate_table,
    span_order,
    noise_step,
    context_mask,
):
    spans, members = lax.axis_size("span"), lax.axis_size("seq")
    chips_y = spans // 2
    ring_x = 4
    ring_z = members // ring_x
    tokens, columns = query.shape[1:]
    length = tokens * members
    dma = pltpu.SemaphoreType.DMA
    in_hbm = pl.BlockSpec(memory_space=pltpu.HBM)
    bf16, f32 = jnp.bfloat16, jnp.float32
    return pl.pallas_call(
        functools.partial(exchange_and_attend, chips_y, ring_z, ring_x),
        out_shape=jax.ShapeDtypeStruct(query.shape, bf16),
        in_specs=[in_hbm] * 11,
        out_specs=in_hbm,
        scratch_shapes=[
            pltpu.VMEM((2, columns), f32),
            pltpu.SMEM(span_order.shape, jnp.int32),
            pltpu.SMEM(noise_step.shape, jnp.int32),
            pltpu.SMEM(context_mask.shape, jnp.int32),
            pltpu.VMEM((2, tokens, columns), bf16),
            pltpu.VMEM((2, tokens, columns), bf16),
            pltpu.VMEM((2, tokens, HD), f32),
            pltpu.VMEM((gate_table.shape[0], HD), f32),
            pltpu.SMEM((2, len(BLOCKS)), f32),
            pltpu.VMEM((length, HD), bf16),
            pltpu.VMEM((HD, length), bf16),
            pltpu.VMEM((len(BLOCKS) + 2, 2, length, HD), bf16),
            pltpu.VMEM((2, length // HALVES, length), f32),
            pltpu.VMEM((length, length), f32),
            pltpu.VMEM((HD, length), f32),
            pltpu.VMEM((1, length), f32),
            pltpu.VMEM((1, length), f32),
            pltpu.VMEM((length, HD), bf16),
            dma((8,)),
            dma((6,)),
            dma,
            dma,
            dma((2,)),
            dma((ring_z,)),
            dma((3,)),
            dma((3,)),
            dma((2,)),
            dma((2, ring_z)),
            dma((2,)),
            dma((2, ring_z)),
            dma((chips_y,)),
            dma((chips_y, HALVES)),
            dma,
            dma,
        ],
        compiler_params=pltpu.CompilerParams(
            collective_id=0, has_side_effects=True, vmem_limit_bytes=63 << 20
        ),
        name="exchange_and_attend",
    )(
        query,
        key,
        value,
        cache_key,
        cache_value,
        q_gain,
        k_gain,
        gate_table,
        span_order,
        noise_step,
        context_mask,
    )


def solution(mesh):
    placed = (
        P("span", "seq", "mp"),
        P("span", "seq", "mp"),
        P("span", "seq", "mp"),
        P("span", "seq", "mp"),
        P("span", "seq", "mp"),
        P("mp"),
        P("mp"),
        P(None, "mp"),
        P(),
        P(),
        P(),
    )
    return jax.shard_map(
        shards, mesh=mesh, in_specs=placed, out_specs=P("span", "seq", "mp"), check_vma=False
    )
```

```python
import functools
import math

import jax
import jax.numpy as jnp
from jax import lax
from jax.experimental import pallas as pl
from jax.experimental.pallas import tpu as pltpu
from jax.sharding import PartitionSpec as P

MESH = pl.DeviceIdType.MESH
HEADS = 32
HD = 128
EPS = 1e-6
Z_ORDER = (0, 1, 3, 2)
HALVES = 2
BLOCKS = ((0, 1), (1, 0), (3, 0), (1, 1), (3, 1), (2, 0), (2, 1))
OWN = len(BLOCKS)
STAGED = OWN + 1
NEAR = (2, 1)
FAR = 5
ONES = 16
WAITS = (
    (1, (("core", 1, 0),)),
    (2, (("core", 2, 0), ("far", 2))),
    (4, (("core", 3, 0), ("far", 3))),
    (6, (("core", 0, 1),)),
    (9, (("core", 1, 1),)),
    (10, (("core", 2, 1),)),
    (12, (("core", 3, 1),)),
)
PIECES = 4
OUT_OF_MAX = 1e30
OUT_OF_SUM = 3e30


def exchange_and_attend(
    chips_y,
    ring_z,
    ring_x,
    query,
    key,
    value,
    cache_key,
    cache_value,
    q_gain,
    k_gain,
    gate_table,
    span_order,
    noise_step,
    context_mask,
    out,
    gains,
    order,
    noise,
    mask,
    raw,
    normed,
    squares,
    gates,
    hide,
    queries,
    queries_t,
    blocks,
    scores,
    own_scores,
    total,
    top,
    mass,
    done,
    load_sem,
    local_sem,
    mp_send,
    mp_recv,
    cache_send,
    cache_recv,
    head_send,
    head_recv,
    near_send,
    near_recv,
    far_send,
    far_recv,
    core_send,
    core_recv,
    out_send,
    out_recv,
):
    span = lax.axis_index("span")
    seq = lax.axis_index("seq")
    mp = lax.axis_index("mp")
    y, core = span // 2, span % 2
    z, x = seq // ring_x, seq % ring_x
    members = ring_z * ring_x
    tokens = raw.shape[1]
    group = ring_x * tokens
    length = members * tokens
    width = HEADS * HD
    partner = (y * 2 + (1 - core), seq, mp)
    my_rows = pl.ds(pl.multiple_of(seq * tokens, tokens), tokens)
    my_columns = pl.ds(pl.multiple_of(seq * HD, HD), HD)

    def peer(dz, dx):
        return lax.rem(z + dz, ring_z) * ring_x + lax.rem(x + dx, ring_x)

    def stage_rows(stage):
        return pl.ds(stage * group, group)

    def landing(stage):
        return pl.ds(pl.multiple_of(stage * group + x * tokens, tokens), tokens)

    barrier = pltpu.get_barrier_semaphore()

    def greet(step, carry):
        other = lax.rem(seq + step, members)
        pl.semaphore_signal(barrier, inc=1, device_id=(span, other, mp), device_id_type=MESH)
        return carry

    lax.fori_loop(1, members, greet, 0)
    for dy in range(1, chips_y):
        pl.semaphore_signal(
            barrier,
            inc=1,
            device_id=(lax.rem(y + dy, chips_y) * 2 + core, seq, mp),
            device_id_type=MESH,
        )
    pl.semaphore_signal(barrier, inc=1, device_id=partner, device_id_type=MESH)
    pl.semaphore_signal(barrier, inc=1, device_id=(span, seq, 1 - mp), device_id_type=MESH)

    loads = [
        pltpu.make_async_copy(source, target, load_sem.at[index])
        for index, (source, target) in enumerate(
            (
                (query.at[0], raw.at[0]),
                (key.at[0], raw.at[1]),
                (q_gain, gains.at[0]),
                (k_gain, gains.at[1]),
                (gate_table.at[:, my_columns], gates),
                (span_order, order),
                (noise_step, noise),
                (context_mask, mask),
            )
        )
    ]
    for load in loads[2:]:
        load.start()
    for which, source in enumerate((query, key)):
        for piece in range(PIECES):
            rows = pl.ds(piece * (tokens // PIECES), tokens // PIECES)
            pltpu.make_async_copy(
                source.at[0, rows], raw.at[which, rows], load_sem.at[which]
            ).start()
    loads[0].wait()
    loads[1].wait()
    lane = lax.broadcasted_iota(jnp.int32, (tokens, HD), 1)

    def row_squares(which):
        wide = raw[which].astype(jnp.float32)
        return jnp.sum(wide * wide, axis=-1, keepdims=True)

    squares[0] = jnp.where(lane < HD // 2, row_squares(0), row_squares(1))
    owns = [
        pltpu.make_async_copy(
            cache_key.at[0, :, my_columns], blocks.at[STAGED, 0, landing(0)], local_sem.at[0]
        ),
        pltpu.make_async_copy(
            cache_value.at[0, :, my_columns], blocks.at[STAGED, 1, landing(0)], local_sem.at[1]
        ),
        pltpu.make_async_copy(value.at[0, :, my_columns], blocks.at[OWN, 1, landing(0)], local_sem.at[2]),
    ]
    for own in owns:
        own.start()
    pl.semaphore_wait(barrier, members - 1 + chips_y - 1 + 2)
    swap = pltpu.make_async_remote_copy(
        src_ref=squares.at[0],
        dst_ref=squares.at[1],
        send_sem=mp_send,
        recv_sem=mp_recv,
        device_id=(span, seq, 1 - mp),
        device_id_type=MESH,
    )
    swap.start()

    def send_caches(stage):
        dz = Z_ORDER[stage]

        def send(dx, carry):
            other = peer(dz, dx)
            columns = pl.ds(pl.multiple_of(other * HD, HD), HD)
            for which in range(2):
                pltpu.make_async_remote_copy(
                    src_ref=(cache_key, cache_value)[which].at[0, :, columns],
                    dst_ref=blocks.at[STAGED, which, landing(stage)],
                    send_sem=cache_send.at[which],
                    recv_sem=cache_recv.at[stage],
                    device_id=(span, other, mp),
                    device_id_type=MESH,
                ).start()
            return carry

        lax.fori_loop(1 if dz == 0 else 0, ring_x, send, 0)

    for stage in range(ring_z):
        send_caches(stage)

    def to_core(source, target, stage, index):
        pltpu.make_async_remote_copy(
            src_ref=blocks.at[source, :, stage_rows(stage)],
            dst_ref=blocks.at[target, :, stage_rows(stage)],
            send_sem=core_send.at[index],
            recv_sem=core_recv.at[index, stage * HALVES // ring_z],
            device_id=partner,
            device_id_type=MESH,
        ).start()

    def along_y(way):
        return (lax.rem(y + (1, chips_y - 1)[way], chips_y) * 2 + core, seq, mp)

    def pass_near(stage):
        for way, place in enumerate(NEAR):
            part = blocks.at[place, :, stage_rows(stage)]
            pltpu.make_async_copy(part, part, near_recv.at[way, stage]).wait()
            pltpu.make_async_remote_copy(
                src_ref=blocks.at[place, way, stage_rows(stage)],
                dst_ref=blocks.at[FAR, way, stage_rows(stage)],
                send_sem=far_send.at[way],
                recv_sem=far_recv.at[way, stage],
                device_id=along_y(way),
                device_id_type=MESH,
            ).start()
            to_core(place, place + 2, stage, place)

    def pass_far(stage):
        for way in range(2):
            part = blocks.at[FAR, way, stage_rows(stage)]
            pltpu.make_async_copy(part, part, far_recv.at[way, stage]).wait()
        to_core(FAR, FAR + 1, stage, 3)

    def await_core(index, half):
        rows = pl.ds(half * (length // HALVES), length // HALVES)
        part = blocks.at[(0, 3, 4, 6)[index], :, rows]
        pltpu.make_async_copy(part, part, core_recv.at[index, half]).wait()

    owns[0].wait()
    owns[1].wait()
    def pass_staged(stage):
        count = (ring_x - 1 if Z_ORDER[stage] == 0 else ring_x) * tokens
        arrived = blocks.at[STAGED, :, pl.ds(0, count)]
        pltpu.make_async_copy(arrived, arrived, cache_recv.at[stage]).wait()
        for way, place in enumerate(NEAR):
            pltpu.make_async_remote_copy(
                src_ref=blocks.at[STAGED, :, stage_rows(stage)],
                dst_ref=blocks.at[place, :, stage_rows(stage)],
                send_sem=near_send.at[way],
                recv_sem=near_recv.at[way, stage],
                device_id=along_y(way),
                device_id_type=MESH,
            ).start()
        to_core(STAGED, 0, stage, 0)

    pass_staged(0)

    swap.wait()
    loads[2].wait()
    loads[3].wait()
    factors = lax.rsqrt((squares[0] + squares[1]) / width + EPS)
    scale = math.log2(math.e) / math.sqrt(HD)

    def send_heads(which, source):
        for stage, dz in enumerate(Z_ORDER):

            def send(dx, carry, stage=stage, dz=dz):
                other = peer(dz, dx)
                columns = pl.ds(pl.multiple_of(other * HD, HD), HD)
                if which == 0:
                    target = queries.at[my_rows]
                else:
                    target = blocks.at[OWN, which - 1, landing(stage)]
                pltpu.make_async_remote_copy(
                    src_ref=source.at[:, columns],
                    dst_ref=target,
                    send_sem=head_send.at[which],
                    recv_sem=head_recv.at[which],
                    device_id=(span, other, mp),
                    device_id_type=MESH,
                ).start()
                return carry

            lax.fori_loop(1 if dz == 0 else 0, ring_x, send, 0)

    for which in range(2):
        at = which * (HD // 2)
        factor = factors[:, at : at + 1] * (scale if which == 0 else 1.0)
        normed[which] = (
            raw[which].astype(jnp.float32) * factor * gains[which][None, :]
        ).astype(jnp.bfloat16)
        own = pltpu.make_async_copy(
            normed.at[which, :, my_columns],
            queries.at[my_rows] if which == 0 else blocks.at[OWN, 0, landing(0)],
            local_sem.at[3 + which],
        )
        own.start()
        owns.append(own)
        send_heads(which, normed.at[which])
    send_heads(2, value.at[0])

    pass_staged(1)
    pass_near(0)
    pass_staged(2)
    pass_near(1)
    pass_far(0)
    pass_staged(3)
    pass_near(2)
    pass_far(1)
    pass_near(3)

    for load in loads[4:8]:
        load.wait()
    for place, (dy, dc) in enumerate(BLOCKS):
        other = lax.rem(y + dy, chips_y) * 2 + lax.rem(core + dc, 2)
        mine, theirs = order[span], order[other]
        seen = jnp.where(theirs < mine, mask[mine, theirs], 0)
        hide[0, place] = jnp.where(seen > 0, 0.0, OUT_OF_MAX).astype(jnp.float32)
        hide[1, place] = jnp.where(seen > 0, 0.0, OUT_OF_SUM).astype(jnp.float32)

    span_rows = length // HALVES
    count = HALVES * len(BLOCKS)

    def rows_of(half):
        return pl.ds(pl.multiple_of(half * span_rows, span_rows), span_rows)

    def score(index, slot, columns):
        scores[slot, :, columns] = jnp.dot(
            blocks[lax.rem(index, len(BLOCKS)), 0, rows_of(index // len(BLOCKS))],
            queries_t[:, columns],
            preferred_element_type=jnp.float32,
        )

    def with_ones(values):
        return jnp.concatenate([values.T, jnp.ones((ONES, values.shape[0]), jnp.bfloat16)], axis=0)

    def weigh(block, columns, values, hide_max, hide_sum):
        before = top[:, columns]
        now = jnp.maximum(before, jnp.max(block, axis=0, keepdims=True) - hide_max)
        weights = jnp.exp2(block - (now + hide_sum)).astype(jnp.bfloat16)
        shrink = jnp.exp2(before - now)
        sums = jnp.dot(values, weights, preferred_element_type=jnp.float32)
        top[:, columns] = now
        mass[:, columns] = mass[:, columns] * shrink + sums[HD : HD + 1]
        total[:, columns] = total[:, columns] * shrink + sums[:HD]

    def weigh_at(index, slot, columns, values):
        place = lax.rem(index, len(BLOCKS))
        weigh(scores[slot, :, columns], columns, values, hide[0, place], hide[1, place])

    def values_at(index):
        return with_ones(blocks[lax.rem(index, len(BLOCKS)), 1, rows_of(index // len(BLOCKS))])

    top[...] = jnp.full_like(top, -3e38)
    mass[...] = jnp.zeros_like(mass)
    total[...] = jnp.zeros_like(total)
    sent = queries.at[pl.ds(0, length - tokens)]
    owns[3].wait()
    pltpu.make_async_copy(sent, sent, head_recv.at[0]).wait()
    queries_t[...] = queries[...].T
    await_core(0, 0)
    parts = [pl.ds(index * 2 * group, 2 * group) for index in range(ring_z // 2)]
    for columns in parts:
        score(0, 0, columns)

    passing = {"staged": pass_staged, "near": pass_near, "far": pass_far, "core": await_core}

    def one_step(index, slot):
        for when, todo in WAITS:
            if when % 2 == slot:

                @pl.when(index == when)
                def _(todo=todo):
                    for what, *which in todo:
                        passing[what](*which)

        values = values_at(index)
        for columns in parts:
            score(index + 1, 1 - slot, columns)
            weigh_at(index, slot, columns, values)

    def two_steps(pair, carry):
        one_step(2 * pair, 0)
        one_step(2 * pair + 1, 1)
        return carry

    lax.fori_loop(0, count // 2 - 1, two_steps, 0)
    one_step(jnp.int32(count - 2), 0)
    owns[4].wait()
    pltpu.make_async_copy(sent, sent, head_recv.at[1]).wait()
    values = values_at(jnp.int32(count - 1))
    for columns in parts:
        own_scores[:, columns] = jnp.dot(
            blocks[OWN, 0], queries_t[:, columns], preferred_element_type=jnp.float32
        )
        weigh_at(jnp.int32(count - 1), 1, columns, values)

    owns[2].wait()
    pltpu.make_async_copy(sent, sent, head_recv.at[2]).wait()
    steps = lax.broadcasted_iota(jnp.int32, gates.shape, 0)
    gate = jnp.sum(jnp.where(steps == noise[span], gates[...], 0.0), axis=0, keepdims=True)
    values = with_ones(blocks[OWN, 1])
    for dz in (2, 1, 3, 0):
        rows = pl.ds(pl.multiple_of(lax.rem(z + dz, ring_z) * group, group), group)
        weigh(own_scores[:, rows], rows, values, 0.0, 0.0)
        attended = total[:, rows] / mass[:, rows]
        factor = lax.rsqrt(jnp.mean(attended * attended, axis=0, keepdims=True) + EPS)
        done[rows] = ((attended * factor).T * gate).astype(jnp.bfloat16)

        def send_out(dx, carry, dz=dz):
            other = peer(dz, dx)
            pltpu.make_async_remote_copy(
                src_ref=done.at[pl.ds(pl.multiple_of(other * tokens, tokens), tokens)],
                dst_ref=out.at[0, :, my_columns],
                send_sem=out_send,
                recv_sem=out_recv,
                device_id=(span, other, mp),
                device_id_type=MESH,
            ).start()
            return carry

        lax.fori_loop(1 if dz == 0 else 0, ring_x, send_out, 0)
    keep = pltpu.make_async_copy(done.at[my_rows], out.at[0, :, my_columns], local_sem.at[5])
    keep.start()
    keep.wait()

    for sem in (cache_send.at[0], cache_send.at[1], head_send.at[0], head_send.at[1], head_send.at[2]):
        pltpu.make_async_copy(sent, sent, sem).wait()
    whole = blocks.at[STAGED]
    for way in range(2):
        pltpu.make_async_copy(whole, whole, near_send.at[way]).wait()
        pltpu.make_async_copy(whole.at[0], whole.at[0], far_send.at[way]).wait()
    for index in range(chips_y):
        pltpu.make_async_copy(whole, whole, core_send.at[index]).wait()
    pltpu.make_async_copy(sent, sent, out_send).wait()
    pltpu.make_async_copy(sent, sent, out_recv).wait()


def shards(
    query,
    key,
    value,
    cache_key,
    cache_value,
    q_gain,
    k_gain,
    gate_table,
    span_order,
    noise_step,
    context_mask,
):
    spans, members = lax.axis_size("span"), lax.axis_size("seq")
    chips_y = spans // 2
    ring_x = 4
    ring_z = members // ring_x
    tokens, columns = query.shape[1:]
    length = tokens * members
    dma = pltpu.SemaphoreType.DMA
    in_hbm = pl.BlockSpec(memory_space=pltpu.HBM)
    bf16, f32 = jnp.bfloat16, jnp.float32
    return pl.pallas_call(
        functools.partial(exchange_and_attend, chips_y, ring_z, ring_x),
        out_shape=jax.ShapeDtypeStruct(query.shape, bf16),
        in_specs=[in_hbm] * 11,
        out_specs=in_hbm,
        scratch_shapes=[
            pltpu.VMEM((2, columns), f32),
            pltpu.SMEM(span_order.shape, jnp.int32),
            pltpu.SMEM(noise_step.shape, jnp.int32),
            pltpu.SMEM(context_mask.shape, jnp.int32),
            pltpu.VMEM((2, tokens, columns), bf16),
            pltpu.VMEM((2, tokens, columns), bf16),
            pltpu.VMEM((2, tokens, HD), f32),
            pltpu.VMEM((gate_table.shape[0], HD), f32),
            pltpu.SMEM((2, len(BLOCKS)), f32),
            pltpu.VMEM((length, HD), bf16),
            pltpu.VMEM((HD, length), bf16),
            pltpu.VMEM((len(BLOCKS) + 2, 2, length, HD), bf16),
            pltpu.VMEM((2, length // HALVES, length), f32),
            pltpu.VMEM((length, length), f32),
            pltpu.VMEM((HD, length), f32),
            pltpu.VMEM((1, length), f32),
            pltpu.VMEM((1, length), f32),
            pltpu.VMEM((length, HD), bf16),
            dma((8,)),
            dma((6,)),
            dma,
            dma,
            dma((2,)),
            dma((ring_z,)),
            dma((3,)),
            dma((3,)),
            dma((2,)),
            dma((2, ring_z)),
            dma((2,)),
            dma((2, ring_z)),
            dma((chips_y,)),
            dma((chips_y, HALVES)),
            dma,
            dma,
        ],
        compiler_params=pltpu.CompilerParams(
            collective_id=0, has_side_effects=True, vmem_limit_bytes=63 << 20
        ),
        name="exchange_and_attend",
    )(
        query,
        key,
        value,
        cache_key,
        cache_value,
        q_gain,
        k_gain,
        gate_table,
        span_order,
        noise_step,
        context_mask,
    )


def solution(mesh):
    placed = (
        P("span", "seq", "mp"),
        P("span", "seq", "mp"),
        P("span", "seq", "mp"),
        P("span", "seq", "mp"),
        P("span", "seq", "mp"),
        P("mp"),
        P("mp"),
        P(None, "mp"),
        P(),
        P(),
        P(),
    )
    return jax.shard_map(
        shards, mesh=mesh, in_specs=placed, out_specs=P("span", "seq", "mp"), check_vma=False
    )
```
